512 devices in a mesh: row: 64 (over z, y_lo, core), rep: 8 (over x, y_hi).
Axes of the slice: x: 4, y: 8 (y_hi: 2, y_lo: 4; y = y_hi * 4 + y_lo), z: 8, core: 2. Of those that a mesh axis runs over, the one named last changes fastest.
Arguments:
- position: float32 [3, 262144], P(None, ('row', 'rep')), may hold values from -4 to 4
- velocity: float32 [3, 262144], P(None, ('row', 'rep')), may hold values from -3 to 3
- acceleration: float32 [3, 262144], P(None, ('row', 'rep')), may hold values from -12 to 12
- star_jerk: float32 [3, 262144], P(None, ('row', 'rep')), may hold values from -48 to 48
- star_mass: float32 [262144], P(('row', 'rep')), may hold values from 3.8146973e-06 to 6.1035156e-05
- time_last: float32 [262144], P(('row', 'rep')), may hold values from -0.25 to -0.05
- first_active: int32 [2048], replicated, may hold values from 0 to 262143, as said below
- second_active: int32 [2048], replicated, may hold values from 0 to 262143, as said below
Outputs:
- final_position: float32 [3, 262144], P(None, ('row', 'rep'))
- final_velocity: float32 [3, 262144], P(None, ('row', 'rep'))
- final_acceleration: float32 [3, 262144], P(None, ('row', 'rep'))
- final_jerk: float32 [3, 262144], P(None, ('row', 'rep'))
The draws below stay inside these ranges and needn't reach their ends.
Inputs may be any that keep to these rules, and one draw needn't show every extreme that they name: `first_active`: 2048 distinct star indices; 0 and 262143 are always among them. `second_active`: 2048 distinct star indices; 0 and 262143 are always among them.
All inputs are finite; a program needn't handle non-finite values.
Results may differ from the reference program's by a relative error of at most 0.0003.
Values sent between devices are 32-bit elements; how exact they have to be, the bound alone decides.
A program may use at most 64 MiB of HBM per device.

```python
import math
import jax
import jax.numpy as jnp
from jax import lax

NSTARS = 262144
ACT = 2048


def choose_active(key):
    key_middle = jax.random.fold_in(key, 1)
    key_order = jax.random.fold_in(key, 2)
    middle_ids = jax.random.permutation(key_middle, NSTARS - 2)[:ACT - 2] + 1
    ends_ids = jnp.array([0, NSTARS - 1], jnp.int32)
    whole_list = jnp.concatenate([ends_ids, middle_ids.astype(jnp.int32)])
    return jax.random.permutation(key_order, whole_list).astype(jnp.int32)


def draw_first_active(key, part):
    key = jax.random.fold_in(key, 11)
    return choose_active(key)


def draw_second_active(key, part):
    key = jax.random.fold_in(key, 23)
    return choose_active(key)


def levels(own_key, shape, shards, smallest, largest):
    level, own = 1.0, jax.random.fold_in(own_key, 6)
    for axis_at, blocks in shards:
        draws = jnp.exp(jax.random.uniform(jax.random.fold_in(own, axis_at), (blocks,), jnp.float32, smallest / len(shards), largest / len(shards)))
        level = level * jnp.repeat(draws, shape[axis_at] // blocks).reshape([-1 if axis == axis_at else 1 for axis in range(len(shape))])
    return level


def bell_draw(rng, dims, scale, most, cuts=(), dtype=jnp.bfloat16):
    factor_of = levels(rng, dims, cuts, -0.22, 0.18) if cuts else 1.0
    values = jax.random.normal(rng, dims, jnp.float32) * scale * factor_of
    return jnp.minimum(jnp.maximum(values, -most), most).astype(dtype)


def setup_inputs(seed: int = 0) -> dict:
    key_of = jax.random.split(jax.random.key(seed), 9)
    position = bell_draw(key_of[0], (3, NSTARS), 1.0, 4.0, ((1, 512),), jnp.float32)
    velocity = bell_draw(key_of[1], (3, NSTARS), 0.5, 3.0, ((1, 512),), jnp.float32)
    acceleration = bell_draw(key_of[2], (3, NSTARS), 2.0, 12.0, ((1, 512),), jnp.float32)
    star_jerk = bell_draw(key_of[3], (3, NSTARS), 8.0, 48.0, ((1, 512),), jnp.float32)
    star_mass = jnp.clip(jnp.exp(math.log(6.103515625e-05) - 2.7725887 * jax.random.uniform(key_of[4], (NSTARS,), jnp.float32) ** levels(key_of[4], (NSTARS,), ((0, 512),), -0.2, 0.2)), 3.814697265625e-06, 6.103515625e-05)
    time_last = jnp.clip(-0.25 + 0.2 * jax.random.uniform(key_of[5], (NSTARS,), jnp.float32) ** levels(key_of[5], (NSTARS,), ((0, 512),), -0.2, 0.2), -0.25, -0.05)
    first_active = draw_first_active(jax.random.fold_in(key_of[8], 71), 0)
    second_active = draw_second_active(jax.random.fold_in(key_of[8], 71), 0)
    return dict(position=position, velocity=velocity, acceleration=acceleration, star_jerk=star_jerk, star_mass=star_mass, time_last=time_last, first_active=first_active, second_active=second_active)


EPS_SQ = 0.0004
STEP_TIMES = (0.0, 0.03125)

def predict(states, step_dt):
    posit = states[0:3]
    veloc = states[3:6]
    accel = states[6:9]
    change = states[9:12]
    pred_pos = posit + step_dt * (veloc + step_dt * (0.5 * accel + step_dt * change / 6.0))
    pred_vel = veloc + step_dt * (accel + step_dt * 0.5 * change)
    return (pred_pos, pred_vel)

def pair_terms(i_pos, i_vel, source):
    offset = source[0:3, None, :] - i_pos[:, :, None]
    relvel = source[3:6, None, :] - i_vel[:, :, None]
    dist_sq = lax.optimization_barrier(jnp.sum(offset * offset, axis=0)) + EPS_SQ
    inverse = lax.rsqrt(dist_sq)
    inv_sq = inverse * inverse
    weight = source[6][None, :] * inverse * inv_sq
    radial = lax.optimization_barrier(jnp.sum(offset * relvel, axis=0)) * inv_sq
    accel = lax.optimization_barrier(jnp.sum(weight[None] * offset, axis=2))
    change = lax.optimization_barrier(jnp.sum(weight[None] * (relvel - 3.0 * radial[None] * offset), axis=2))
    return (accel, change)

def sum_blocks(i_pos, i_vel, source, width):
    columns = source.shape[1]
    if columns > width and columns % width == 0:
        blocks = source.reshape(7, columns // width, width).transpose(1, 0, 2)

        def add_block(totals, block_data):
            accel, change = pair_terms(i_pos, i_vel, block_data)
            return ((totals[0] + accel, totals[1] + change), None)
        empty_sum = jnp.zeros(i_pos.shape, jnp.float32)
        totals, unused = lax.scan(add_block, (empty_sum, empty_sum), blocks)
        return totals
    return pair_terms(i_pos, i_vel, source)

def correct(initial, accel_new, jerk_new, t_now):
    posit = initial[0:3]
    veloc = initial[3:6]
    accel = initial[6:9]
    change = initial[9:12]
    step_dt = t_now - initial[12]
    vel_new = veloc + 0.5 * step_dt * (accel + accel_new) + step_dt * step_dt * (change - jerk_new) / 12.0
    pos_new = posit + 0.5 * step_dt * (veloc + vel_new) + step_dt * step_dt * (accel - accel_new) / 12.0
    return jnp.concatenate([pos_new, vel_new, accel_new, jerk_new], axis=0)

def reference(position, velocity, acceleration, star_jerk, star_mass, time_last, first_active, second_active):
    states = jnp.concatenate([position, velocity, acceleration, star_jerk], axis=0)
    time_now = time_last
    for t_now, active in ((STEP_TIMES[0], first_active), (STEP_TIMES[1], second_active)):
        pred_pos, pred_vel = predict(states, t_now - time_now)
        source = jnp.concatenate([pred_pos, pred_vel, star_mass[None]], axis=0)
        initial = jnp.concatenate([states, time_now[None]], axis=0)[:, active]
        i_pos, i_vel = predict(initial[0:12], t_now - initial[12])
        accel_new, jerk_new = sum_blocks(i_pos, i_vel, source, 1024)
        updated = correct(initial, accel_new, jerk_new, t_now)
        states = states.at[:, active].set(updated)
        time_now = time_now.at[active].set(t_now)
    return (states[0:3], states[3:6], states[6:9], states[9:12])
```

```python
import functools

import jax
import jax.numpy as jnp
from jax import lax
from jax.experimental import pallas as pl
from jax.experimental.pallas import tpu as pltpu
from jax.sharding import PartitionSpec as P

MESH = pl.DeviceIdType.MESH
F32 = jnp.float32
BF16 = jnp.bfloat16
EPS_SQ = 0.0004
T_ONE = 0.0
T_TWO = 0.03125
ACT = 2048
OWN = 512
LANES = 128
SLICES = 16
BLOCKS = 32


def place():
    row, rep = lax.axis_index("row"), lax.axis_index("rep")
    slice_at = (row // 8) * 2 + row % 2
    block_at = (rep // 2) * 8 + (rep % 2) * 4 + (row // 2) % 4
    return slice_at, block_at


def device_of(slice_at, block_at):
    y = block_at % 8
    row = ((slice_at // 2) * 4 + y % 4) * 2 + slice_at % 2
    return row, (block_at // 8) * 2 + y // 4


def slice_peer(i, slice_at):
    half = (i + 1) // 2
    return (slice_at + 8 + half * (2 * (i % 2) - 1) + SLICES) % SLICES


def block_peer(i, block_at):
    j, k = i // 8, i % 8
    x_step = (1 - j // 2) * (2 + j) + (j // 2) * (3 - j)
    y_step = 4 + ((k + 1) // 2) * (2 * (k % 2) - 1)
    x = (block_at // 8 + x_step) % 4
    y = (block_at % 8 + y_step) % 8
    return x * 8 + y


def split_rows(rows):
    high = rows.astype(BF16).astype(F32)
    rest = rows - high
    middle = rest.astype(BF16).astype(F32)
    low = rest - middle
    return jnp.concatenate([high, middle, low, jnp.zeros_like(rows)], axis=0).astype(BF16)


def join_rows(parts):
    return parts[0:8] + (parts[8:16] + parts[16:24])


def pick(rows, match):
    return join_rows(jnp.dot(split_rows(rows), match, preferred_element_type=F32))


def put(rows, match):
    dims = (((1,), (1,)), ((), ()))
    return join_rows(lax.dot_general(split_rows(rows), match, dims, preferred_element_type=F32))


def predict(x, v, a, j, h):
    return (x + h * (v + h * (0.5 * a + h * j / 6.0)), v + h * (a + h * 0.5 * j))


def corrector_base(x, v, a, j, h):
    v_base = v + 0.5 * h * a + h * h * j / 12.0
    x_base = x + 0.5 * h * (v + v_base) + h * h * a / 12.0
    return x_base, v_base


def corrector_rest(x_base, v_base, a_new, j_new, h):
    v_new = v_base + 0.5 * h * a_new - h * h * j_new / 12.0
    x_new = x_base + (h * h / 6.0) * a_new - (h * h * h / 24.0) * j_new
    return x_new, v_new


def forces(i_rows, source, extra, i_wide, sums):
    columns = jnp.transpose(i_rows)
    for c in range(6):
        i_wide[c] = jnp.broadcast_to(columns[:, c : c + 1], (LANES, LANES))
    groups = 4

    def add_pairs(star, total, src):
        dx, dy, dz = src[0] - star[0], src[1] - star[1], src[2] - star[2]
        ux, uy, uz = src[3] - star[3], src[4] - star[4], src[5] - star[5]
        inverse = lax.rsqrt(dx * dx + dy * dy + (dz * dz + EPS_SQ))
        inv_sq = inverse * inverse
        weight = (src[6] * inverse) * inv_sq
        radial = (dx * ux + dy * uy + dz * uz) * inv_sq
        turn = weight * (3.0 * radial)
        return (
            total[0] + weight * dx,
            total[1] + weight * dy,
            total[2] + weight * dz,
            total[3] + (weight * ux - turn * dx),
            total[4] + (weight * uy - turn * dy),
            total[5] + (weight * uz - turn * dz),
        )

    def some_stars(g, _):
        base = pl.multiple_of(g * (8 * groups), 8 * groups)
        stars = [[i_wide[c, pl.ds(base + 8 * k, 8), :] for c in range(6)] for k in range(groups)]

        def some_sources(t, totals):
            lane = pl.multiple_of((t % 4) * LANES, LANES)
            src = [
                jnp.broadcast_to(source[t // 4, c : c + 1, pl.ds(lane, LANES)], (8, LANES))
                for c in range(7)
            ]
            return tuple(add_pairs(stars[k], totals[k], src) for k in range(groups))

        zero = jnp.zeros((8, LANES), F32)
        totals = lax.fori_loop(0, 64, some_sources, ((zero,) * 6,) * groups, unroll=4)
        if extra is not None:
            src = [jnp.broadcast_to(extra[c : c + 1, :], (8, LANES)) for c in range(7)]
            totals = tuple(add_pairs(stars[k], totals[k], src) for k in range(groups))
        for k in range(groups):
            for c in range(6):
                sums[c, pl.ds(base + 8 * k, 8), :] = totals[k][c]
        return 0

    lax.fori_loop(0, LANES // (8 * groups), some_stars, 0)
    lane = lax.broadcasted_iota(jnp.int32, (LANES, LANES), 1)
    columns = jnp.zeros((LANES, LANES), F32)
    for c in range(6):
        columns = jnp.where(lane == c, jnp.sum(sums[c], axis=1, keepdims=True), columns)
    return jnp.transpose(columns)[0:8]


def kernel(
    pos_ref, vel_ref, acc_ref, jerk_ref, mass_ref, time_ref, first_ref, second_ref,
    out_pos, out_vel, out_acc, out_jerk,
    match_one, match_two, match_both, rows_scr, i_wide, sums,
    pick_one, pick_two, base_mine,
    got_pick, got_base, src_one, src_two, all_pick, all_base,
    part_one, part_two, updated, total_one, total_two,
    send_sem, recv_sem,
):
    slice_at, block_at = place()

    barrier = pltpu.get_barrier_semaphore()

    def greet_block(i, _):
        to = device_of(slice_at, block_peer(i, block_at))
        pl.semaphore_signal(barrier, inc=1, device_id=to, device_id_type=MESH)
        return 0

    def greet_slice(i, _):
        to = device_of(slice_peer(i, slice_at), block_at)
        pl.semaphore_signal(barrier, inc=1, device_id=to, device_id_type=MESH)
        return 0

    lax.fori_loop(0, BLOCKS - 1, greet_block, 0)
    lax.fori_loop(0, SLICES - 1, greet_slice, 0)

    def to_slices(source_of, into, rows, sem):
        def one(i, _):
            peer = slice_peer(i, slice_at)
            pltpu.make_async_remote_copy(
                src_ref=source_of(peer).at[pl.ds(0, rows)],
                dst_ref=into.at[slice_at, pl.ds(0, rows)],
                send_sem=send_sem.at[sem],
                recv_sem=recv_sem.at[sem],
                device_id=device_of(peer, block_at),
                device_id_type=MESH,
            ).start()
            return 0

        lax.fori_loop(0, SLICES - 1, one, 0)

    def to_blocks(into, rows, sem):
        def one(i, _):
            mine = into.at[block_at, pl.ds(0, rows)]
            pltpu.make_async_remote_copy(
                src_ref=mine,
                dst_ref=mine,
                send_sem=send_sem.at[sem],
                recv_sem=recv_sem.at[sem],
                device_id=device_of(slice_at, block_peer(i, block_at)),
                device_id_type=MESH,
            ).start()
            return 0

        lax.fori_loop(0, BLOCKS - 1, one, 0)

    def wait(sems, buffer, rows, sem):
        whole = buffer.at[pl.ds(0, buffer.shape[0] - 1), pl.ds(0, rows)]
        pltpu.make_async_copy(whole, whole, sems.at[sem]).wait()

    pos, vel, acc, jerk = pos_ref[...], vel_ref[...], acc_ref[...], jerk_ref[...]
    time = jnp.concatenate([time_ref[k : k + 1, :] for k in range(4)], axis=1)
    mass = jnp.concatenate([mass_ref[k : k + 1, :] for k in range(4)], axis=1)
    base_id = (lax.axis_index("row") * 8 + lax.axis_index("rep")) * OWN
    owned = lax.broadcasted_iota(jnp.int32, (OWN, LANES), 0) + base_id

    def fill_match(match, ids):
        for q in range(SLICES):
            hit = jnp.broadcast_to(ids[q : q + 1, :], (OWN, LANES)) == owned
            match[:, q * LANES : (q + 1) * LANES] = jnp.where(hit, 1.0, 0.0).astype(BF16)

    fill_match(match_one, first_ref)
    h_one = T_ONE - time
    pred_pos, pred_vel = predict(pos, vel, acc, jerk, h_one)
    rows_scr[0:3, :] = pred_pos
    rows_scr[3:6, :] = pred_vel
    rows_scr[6:7, :] = mass
    rows_scr[7:8, :] = jnp.zeros_like(mass)
    rows = rows_scr[...]
    src_one[slice_at] = rows
    picked = pick(rows, match_one[...])
    for q in range(SLICES):
        pick_one[q] = picked[:, q * LANES : (q + 1) * LANES]
    got_pick[slice_at] = pick_one[slice_at]

    pl.semaphore_wait(barrier, SLICES + BLOCKS - 2)
    to_slices(lambda peer: pick_one.at[peer], got_pick, 6, 0)
    to_slices(lambda peer: src_one.at[slice_at], src_one, 8, 1)

    x_base, v_base = corrector_base(pos, vel, acc, jerk, h_one)
    rows_scr[0:3, :] = x_base
    rows_scr[3:6, :] = v_base
    rows_scr[6:7, :] = h_one
    rows_scr[7:8, :] = mass
    picked = pick(rows_scr[...], match_one[...])
    for q in range(SLICES):
        pick_two[q, 0:8, :] = picked[:, q * LANES : (q + 1) * LANES]
    fill_match(match_two, second_ref)
    pred_pos, pred_vel = predict(pos, vel, acc, jerk, T_TWO - time)
    rows_scr[0:3, :] = pred_pos
    rows_scr[3:6, :] = pred_vel
    rows_scr[6:7, :] = mass
    rows_scr[7:8, :] = jnp.zeros_like(mass)
    picked = pick(rows_scr[...], match_two[...])
    for q in range(SLICES):
        pick_two[q, 8:16, :] = picked[:, q * LANES : (q + 1) * LANES]
    got_base[slice_at] = pick_two[slice_at]
    ones = jnp.ones((16, ACT), BF16)
    dims = (((1,), (1,)), ((), ()))
    hit_one = lax.dot_general(ones, match_one[...], dims, preferred_element_type=F32)[0:1]
    hit_two = lax.dot_general(ones, match_two[...], dims, preferred_element_type=F32)[0:1]
    rows_scr[6:7, :] = jnp.where(hit_one > 0.5, 0.0, mass)
    src_two[slice_at] = rows_scr[...]

    wait(recv_sem, got_pick, 6, 0)
    total = got_pick[0]
    for q in range(1, SLICES):
        total = total + got_pick[q]
    all_pick[block_at] = total
    to_blocks(all_pick, 6, 2)
    to_slices(lambda peer: pick_two.at[peer], got_base, 16, 3)

    mine = jnp.broadcast_to(second_ref[pl.ds(slice_at, 1), :].astype(F32), (LANES, LANES))
    mine = jnp.transpose(mine)
    for q in range(SLICES):
        theirs = jnp.broadcast_to(first_ref[q : q + 1, :].astype(F32), (LANES, LANES))
        hit = jnp.where(mine == theirs, 1.0, 0.0).astype(BF16)
        match_both[:, q * LANES : (q + 1) * LANES] = hit

    wait(recv_sem, src_one, 8, 1)
    wait(recv_sem, all_pick, 6, 2)
    stars_one = all_pick[0]
    for s in range(1, BLOCKS):
        stars_one = stars_one + all_pick[s]

    wait(recv_sem, got_base, 16, 3)
    total = got_base[0]
    for q in range(1, SLICES):
        total = total + got_base[q]
    all_base[block_at] = total
    to_blocks(all_base, 16, 4)
    to_slices(lambda peer: src_two.at[slice_at], src_two, 8, 5)

    part_one[block_at] = forces(stars_one, src_one, None, i_wide, sums)
    to_blocks(part_one, 6, 6)

    wait(recv_sem, all_base, 16, 4)
    base = all_base[0]
    for s in range(1, BLOCKS):
        base = base + all_base[s]
    base_mine[...] = base
    wait(recv_sem, part_one, 6, 6)
    total = part_one[0]
    for s in range(1, BLOCKS):
        total = total + part_one[s]
    h = base_mine[6:7, :]
    a_new, j_new = total[0:3], total[3:6]
    x_new, v_new = corrector_rest(base_mine[0:3, :], base_mine[3:6, :], a_new, j_new, h)
    pred_pos, pred_vel = predict(x_new, v_new, a_new, j_new, T_TWO - T_ONE)
    updated[slice_at, 0:3, :] = pred_pos
    updated[slice_at, 3:6, :] = pred_vel
    updated[slice_at, 6:7, :] = base_mine[7:8, :]
    updated[slice_at, 7:8, :] = jnp.ones_like(h)
    to_slices(lambda peer: updated.at[slice_at], updated, 8, 7)
    total_one[slice_at] = total
    to_slices(lambda peer: total_one.at[slice_at], total_one, 6, 8)

    wait(recv_sem, src_two, 8, 5)
    wait(recv_sem, updated, 8, 7)
    moved = jnp.concatenate([updated[q] for q in range(SLICES)], axis=1)
    moved = put(moved, match_both[...])
    stars_two = jnp.where(moved[7:8] > 0.5, moved, base_mine[8:16, :])
    extra = updated[block_at // 2]
    lane = lax.broadcasted_iota(jnp.int32, (8, LANES), 1)
    row = lax.broadcasted_iota(jnp.int32, (8, LANES), 0)
    extra = jnp.where((row == 6) & (lane // 64 != block_at % 2), 0.0, extra)
    part_two[block_at] = forces(stars_two, src_two, extra, i_wide, sums)
    to_blocks(part_two, 6, 9)

    wait(recv_sem, total_one, 6, 8)
    placed = put(jnp.concatenate([total_one[q] for q in range(SLICES)], axis=1), match_one[...])
    was_hit = hit_one > 0.5
    a_new, j_new = placed[0:3], placed[3:6]
    x_new, v_new = corrector_rest(x_base, v_base, a_new, j_new, h_one)
    pos = jnp.where(was_hit, x_new, pos)
    vel = jnp.where(was_hit, v_new, vel)
    acc = jnp.where(was_hit, a_new, acc)
    jerk = jnp.where(was_hit, j_new, jerk)
    h_two = T_TWO - jnp.where(was_hit, T_ONE, time)
    x_base, v_base = corrector_base(pos, vel, acc, jerk, h_two)

    wait(recv_sem, part_two, 6, 9)
    total = part_two[0]
    for s in range(1, BLOCKS):
        total = total + part_two[s]
    total_two[slice_at] = total
    to_slices(lambda peer: total_two.at[slice_at], total_two, 6, 10)
    for sem, buffer, rows in (
        (0, got_pick, 6), (1, src_one, 8), (2, all_pick, 6), (3, got_base, 16), (4, all_base, 16), (5, src_two, 8),
        (6, part_one, 6), (7, updated, 8), (8, total_one, 6), (9, part_two, 6),
    ):
        wait(send_sem, buffer, rows, sem)
    wait(recv_sem, total_two, 6, 10)
    placed = put(jnp.concatenate([total_two[q] for q in range(SLICES)], axis=1), match_two[...])
    was_hit = hit_two > 0.5
    a_new, j_new = placed[0:3], placed[3:6]
    x_new, v_new = corrector_rest(x_base, v_base, a_new, j_new, h_two)
    out_pos[...] = jnp.where(was_hit, x_new, pos)
    out_vel[...] = jnp.where(was_hit, v_new, vel)
    out_acc[...] = jnp.where(was_hit, a_new, acc)
    out_jerk[...] = jnp.where(was_hit, j_new, jerk)
    wait(send_sem, total_two, 6, 10)


def body(position, velocity, acceleration, star_jerk, star_mass, time_last, first_active, second_active):
    vmem = pl.BlockSpec(memory_space=pltpu.VMEM)
    out = jax.ShapeDtypeStruct(position.shape, F32)
    slices = lambda rows, lanes=LANES: pltpu.VMEM((SLICES, rows, lanes), F32)
    blocks = lambda rows: pltpu.VMEM((BLOCKS, rows, LANES), F32)
    return pl.pallas_call(
        kernel,
        out_shape=(out,) * 4,
        in_specs=[vmem] * 8,
        out_specs=(vmem,) * 4,
        scratch_shapes=[
            pltpu.VMEM((OWN, ACT), BF16),
            pltpu.VMEM((OWN, ACT), BF16),
            pltpu.VMEM((LANES, ACT), BF16),
            pltpu.VMEM((8, OWN), F32),
            pltpu.VMEM((6, LANES, LANES), F32),
            pltpu.VMEM((6, LANES, LANES), F32),
            slices(8),
            slices(16),
            pltpu.VMEM((16, LANES), F32),
            slices(8),
            slices(16),
            slices(8, OWN),
            slices(8, OWN),
            blocks(8),
            blocks(16),
            blocks(8),
            blocks(8),
            slices(8),
            slices(8),
            slices(8),
            pltpu.SemaphoreType.DMA((11,)),
            pltpu.SemaphoreType.DMA((11,)),
        ],
        compiler_params=pltpu.CompilerParams(
            collective_id=0, has_side_effects=True, vmem_limit_bytes=40 * 1024 * 1024
        ),
    )(
        position,
        velocity,
        acceleration,
        star_jerk,
        star_mass.reshape(4, LANES),
        time_last.reshape(4, LANES),
        first_active.reshape(SLICES, LANES),
        second_active.reshape(SLICES, LANES),
    )


def solution(mesh):
    split = P(None, ("row", "rep"))
    flat = P(("row", "rep"))
    return jax.shard_map(
        body,
        mesh=mesh,
        in_specs=(split,) * 4 + (flat,) * 2 + (P(),) * 2,
        out_specs=(split,) * 4,
        check_vma=False,
    )
```

```python
import functools

import jax
import jax.numpy as jnp
from jax import lax
from jax.experimental import pallas as pl
from jax.experimental.pallas import tpu as pltpu
from jax.sharding import PartitionSpec as P

MESH = pl.DeviceIdType.MESH
F32 = jnp.float32
BF16 = jnp.bfloat16
EPS_SQ = 0.0004
T_ONE = 0.0
T_TWO = 0.03125
ACT = 2048
OWN = 512
LANES = 128
SLICES = 16
BLOCKS = 32


def place():
    row, rep = lax.axis_index("row"), lax.axis_index("rep")
    slice_at = (row // 8) * 2 + row % 2
    block_at = (rep // 2) * 8 + (rep % 2) * 4 + (row // 2) % 4
    return slice_at, block_at


def peers(slice_at, block_at):
    z, core = slice_at // 2, slice_at % 2
    x, y = block_at // 8, block_at % 8
    row = z * 8 + (y % 4) * 2 + core
    rep = x * 2 + y // 4
    near = (4, 3, 5, 2, 6, 1, 7, 0)
    zs = [(z + k) % 8 for k in near]
    ys = [(y + k) % 8 for k in near]
    xs = [(x + k) % 4 for k in (2, 1, 3, 0)]
    rows = [z * 8 + core + (k % 4) * 2 for k in ys]
    reps = [k // 4 for k in ys]
    others = [(k * 2 + side, (k * 8 + (y % 4) * 2 + side, rep)) for k in zs for side in (1 - core, core)]
    blocks = [(xs[i] * 8 + ys[j], (rows[j], xs[i] * 2 + reps[j])) for i in range(4) for j in range(8)]
    return others[:-1], blocks[:-1]


def split_rows(rows):
    high = rows.astype(BF16).astype(F32)
    rest = rows - high
    middle = rest.astype(BF16).astype(F32)
    low = rest - middle
    return jnp.concatenate([high, middle, low, jnp.zeros_like(rows)], axis=0).astype(BF16)


def join_rows(parts):
    return parts[0:8] + (parts[8:16] + parts[16:24])


def pick(rows, match):
    return join_rows(jnp.dot(split_rows(rows), match, preferred_element_type=F32))


def put(rows, match):
    dims = (((1,), (1,)), ((), ()))
    return join_rows(lax.dot_general(split_rows(rows), match, dims, preferred_element_type=F32))


def predict(x, v, a, j, h):
    return (x + h * (v + h * (0.5 * a + h * j / 6.0)), v + h * (a + h * 0.5 * j))


def corrector_base(x, v, a, j, h):
    v_base = v + 0.5 * h * a + h * h * j / 12.0
    x_base = x + 0.5 * h * (v + v_base) + h * h * a / 12.0
    return x_base, v_base


def corrector_rest(x_base, v_base, a_new, j_new, h):
    v_new = v_base + 0.5 * h * a_new - h * h * j_new / 12.0
    x_new = x_base + (h * h / 6.0) * a_new - (h * h * h / 24.0) * j_new
    return x_new, v_new


def forces(i_rows, source, extra, i_wide, sums):
    columns = jnp.transpose(i_rows)
    for c in range(6):
        i_wide[c] = jnp.broadcast_to(columns[:, c : c + 1], (LANES, LANES))
    groups = 4

    def add_pairs(star, total, src):
        dx, dy, dz = src[0] - star[0], src[1] - star[1], src[2] - star[2]
        ux, uy, uz = src[3] - star[3], src[4] - star[4], src[5] - star[5]
        inverse = lax.rsqrt(dx * dx + dy * dy + (dz * dz + EPS_SQ))
        inv_sq = inverse * inverse
        weight = (src[6] * inverse) * inv_sq
        radial = (dx * ux + dy * uy + dz * uz) * inv_sq
        turn = weight * (3.0 * radial)
        return (
            total[0] + weight * dx,
            total[1] + weight * dy,
            total[2] + weight * dz,
            total[3] + (weight * ux - turn * dx),
            total[4] + (weight * uy - turn * dy),
            total[5] + (weight * uz - turn * dz),
        )

    def some_stars(g, _):
        base = pl.multiple_of(g * (8 * groups), 8 * groups)
        stars = [[i_wide[c, pl.ds(base + 8 * k, 8), :] for c in range(6)] for k in range(groups)]

        def some_sources(t, totals):
            lane = pl.multiple_of((t % 4) * LANES, LANES)
            src = [
                jnp.broadcast_to(source[t // 4, c : c + 1, pl.ds(lane, LANES)], (8, LANES))
                for c in range(7)
            ]
            return tuple(add_pairs(stars[k], totals[k], src) for k in range(groups))

        zero = jnp.zeros((8, LANES), F32)
        totals = lax.fori_loop(0, 64, some_sources, ((zero,) * 6,) * groups, unroll=4)
        if extra is not None:
            src = [jnp.broadcast_to(extra[c : c + 1, :], (8, LANES)) for c in range(7)]
            totals = tuple(add_pairs(stars[k], totals[k], src) for k in range(groups))
        for k in range(groups):
            for c in range(6):
                sums[c, pl.ds(base + 8 * k, 8), :] = totals[k][c]
        return 0

    lax.fori_loop(0, LANES // (8 * groups), some_stars, 0)
    lane = lax.broadcasted_iota(jnp.int32, (LANES, LANES), 1)
    columns = jnp.zeros((LANES, LANES), F32)
    for c in range(6):
        columns = jnp.where(lane == c, jnp.sum(sums[c], axis=1, keepdims=True), columns)
    return jnp.transpose(columns)[0:8]


def kernel(
    pos_hbm, vel_hbm, acc_hbm, jerk_hbm, mass_hbm, time_hbm, first_hbm, second_hbm,
    out_pos, out_vel, out_acc, out_jerk,
    match_one, match_two, match_both, rows_scr, i_wide, sums,
    pick_one, pick_two, base_mine,
    got_pick, got_base, src_one, src_two, all_pick, all_base,
    part_one, part_two, updated, total_one, total_two,
    pos_ref, vel_ref, acc_ref, jerk_ref, mass_ref, time_ref, first_ref, second_ref,
    load_sem, send_sem, recv_sem,
):
    slice_at, block_at = place()
    loads = [
        pltpu.make_async_copy(source, into, load_sem.at[i])
        for i, (source, into) in enumerate((
            (first_hbm, first_ref), (pos_hbm, pos_ref), (vel_hbm, vel_ref), (acc_hbm, acc_ref), (jerk_hbm, jerk_ref),
            (mass_hbm, mass_ref), (time_hbm, time_ref), (second_hbm, second_ref),
        ))
    ]
    for load in loads:
        load.start()

    barrier = pltpu.get_barrier_semaphore()

    other_slices, other_blocks = peers(slice_at, block_at)
    for _, to in other_blocks + other_slices:
        pl.semaphore_signal(barrier, inc=1, device_id=to, device_id_type=MESH)

    def to_slices(source_of, into, rows, sem):
        for peer, to in other_slices:
            pltpu.make_async_remote_copy(
                src_ref=source_of(peer).at[pl.ds(0, rows)],
                dst_ref=into.at[slice_at, pl.ds(0, rows)],
                send_sem=send_sem.at[sem],
                recv_sem=recv_sem.at[sem],
                device_id=to,
                device_id_type=MESH,
            ).start()

    def to_blocks(into, rows, sem):
        mine = into.at[block_at, pl.ds(0, rows)]
        for _, to in other_blocks:
            pltpu.make_async_remote_copy(
                src_ref=mine,
                dst_ref=mine,
                send_sem=send_sem.at[sem],
                recv_sem=recv_sem.at[sem],
                device_id=to,
                device_id_type=MESH,
            ).start()

    def wait(sems, buffer, rows, sem):
        whole = buffer.at[pl.ds(0, buffer.shape[0] - 1), pl.ds(0, rows)]
        pltpu.make_async_copy(whole, whole, sems.at[sem]).wait()

    for load in loads:
        load.wait()
    pos, vel, acc, jerk = pos_ref[...], vel_ref[...], acc_ref[...], jerk_ref[...]
    time = jnp.concatenate([time_ref[k : k + 1, :] for k in range(4)], axis=1)
    mass = jnp.concatenate([mass_ref[k : k + 1, :] for k in range(4)], axis=1)
    base_id = (lax.axis_index("row") * 8 + lax.axis_index("rep")) * OWN
    owned = lax.broadcasted_iota(jnp.int32, (OWN, LANES), 0) + base_id

    def fill_match(match, ids):
        for q in range(SLICES):
            hit = jnp.broadcast_to(ids[q : q + 1, :], (OWN, LANES)) == owned
            match[:, q * LANES : (q + 1) * LANES] = jnp.where(hit, 1.0, 0.0).astype(BF16)

    fill_match(match_one, first_ref)
    h_one = T_ONE - time
    pred_pos, pred_vel = predict(pos, vel, acc, jerk, h_one)
    rows_scr[0:3, :] = pred_pos
    rows_scr[3:6, :] = pred_vel
    rows_scr[6:7, :] = mass
    rows_scr[7:8, :] = jnp.zeros_like(mass)
    rows = rows_scr[...]
    src_one[slice_at] = rows
    picked = pick(rows, match_one[...])
    for q in range(SLICES):
        pick_one[q] = picked[:, q * LANES : (q + 1) * LANES]
    got_pick[slice_at] = pick_one[slice_at]

    pl.semaphore_wait(barrier, SLICES + BLOCKS - 2)
    to_slices(lambda peer: pick_one.at[peer], got_pick, 6, 0)
    to_slices(lambda peer: src_one.at[slice_at], src_one, 8, 1)

    x_base, v_base = corrector_base(pos, vel, acc, jerk, h_one)
    rows_scr[0:3, :] = x_base
    rows_scr[3:6, :] = v_base
    rows_scr[6:7, :] = h_one
    rows_scr[7:8, :] = mass
    picked = pick(rows_scr[...], match_one[...])
    for q in range(SLICES):
        pick_two[q, 0:8, :] = picked[:, q * LANES : (q + 1) * LANES]
    fill_match(match_two, second_ref)
    pred_pos, pred_vel = predict(pos, vel, acc, jerk, T_TWO - time)
    rows_scr[0:3, :] = pred_pos
    rows_scr[3:6, :] = pred_vel
    rows_scr[6:7, :] = mass
    rows_scr[7:8, :] = jnp.zeros_like(mass)
    picked = pick(rows_scr[...], match_two[...])
    for q in range(SLICES):
        pick_two[q, 8:16, :] = picked[:, q * LANES : (q + 1) * LANES]
    got_base[slice_at] = pick_two[slice_at]
    ones = jnp.ones((16, ACT), BF16)
    dims = (((1,), (1,)), ((), ()))
    hit_one = lax.dot_general(ones, match_one[...], dims, preferred_element_type=F32)[0:1]
    hit_two = lax.dot_general(ones, match_two[...], dims, preferred_element_type=F32)[0:1]
    rows_scr[6:7, :] = jnp.where(hit_one > 0.5, 0.0, mass)
    src_two[slice_at] = rows_scr[...]

    wait(recv_sem, got_pick, 6, 0)
    total = got_pick[0]
    for q in range(1, SLICES):
        total = total + got_pick[q]
    all_pick[block_at] = total
    to_blocks(all_pick, 6, 2)
    to_slices(lambda peer: pick_two.at[peer], got_base, 16, 3)

    mine = jnp.broadcast_to(second_ref[pl.ds(slice_at, 1), :].astype(F32), (LANES, LANES))
    mine = jnp.transpose(mine)
    for q in range(SLICES):
        theirs = jnp.broadcast_to(first_ref[q : q + 1, :].astype(F32), (LANES, LANES))
        hit = jnp.where(mine == theirs, 1.0, 0.0).astype(BF16)
        match_both[:, q * LANES : (q + 1) * LANES] = hit

    wait(recv_sem, src_one, 8, 1)
    wait(recv_sem, all_pick, 6, 2)
    stars_one = all_pick[0]
    for s in range(1, BLOCKS):
        stars_one = stars_one + all_pick[s]

    wait(recv_sem, got_base, 16, 3)
    total = got_base[0]
    for q in range(1, SLICES):
        total = total + got_base[q]
    all_base[block_at] = total
    to_blocks(all_base, 16, 4)
    to_slices(lambda peer: src_two.at[slice_at], src_two, 8, 5)

    part_one[block_at] = forces(stars_one, src_one, None, i_wide, sums)
    to_blocks(part_one, 6, 6)

    wait(recv_sem, all_base, 16, 4)
    base = all_base[0]
    for s in range(1, BLOCKS):
        base = base + all_base[s]
    base_mine[...] = base
    wait(recv_sem, part_one, 6, 6)
    total = part_one[0]
    for s in range(1, BLOCKS):
        total = total + part_one[s]
    h = base_mine[6:7, :]
    a_new, j_new = total[0:3], total[3:6]
    x_new, v_new = corrector_rest(base_mine[0:3, :], base_mine[3:6, :], a_new, j_new, h)
    pred_pos, pred_vel = predict(x_new, v_new, a_new, j_new, T_TWO - T_ONE)
    updated[slice_at, 0:3, :] = pred_pos
    updated[slice_at, 3:6, :] = pred_vel
    updated[slice_at, 6:7, :] = base_mine[7:8, :]
    updated[slice_at, 7:8, :] = jnp.ones_like(h)
    to_slices(lambda peer: updated.at[slice_at], updated, 8, 7)
    total_one[slice_at] = total
    to_slices(lambda peer: total_one.at[slice_at], total_one, 6, 8)

    wait(recv_sem, src_two, 8, 5)
    wait(recv_sem, updated, 8, 7)
    moved = jnp.concatenate([updated[q] for q in range(SLICES)], axis=1)
    moved = put(moved, match_both[...])
    stars_two = jnp.where(moved[7:8] > 0.5, moved, base_mine[8:16, :])
    extra = updated[block_at // 2]
    lane = lax.broadcasted_iota(jnp.int32, (8, LANES), 1)
    row = lax.broadcasted_iota(jnp.int32, (8, LANES), 0)
    extra = jnp.where((row == 6) & (lane // 64 != block_at % 2), 0.0, extra)
    part_two[block_at] = forces(stars_two, src_two, extra, i_wide, sums)
    to_blocks(part_two, 6, 9)

    wait(recv_sem, total_one, 6, 8)
    placed = put(jnp.concatenate([total_one[q] for q in range(SLICES)], axis=1), match_one[...])
    was_hit = hit_one > 0.5
    a_new, j_new = placed[0:3], placed[3:6]
    x_new, v_new = corrector_rest(x_base, v_base, a_new, j_new, h_one)
    pos = jnp.where(was_hit, x_new, pos)
    vel = jnp.where(was_hit, v_new, vel)
    acc = jnp.where(was_hit, a_new, acc)
    jerk = jnp.where(was_hit, j_new, jerk)
    h_two = T_TWO - jnp.where(was_hit, T_ONE, time)
    x_base, v_base = corrector_base(pos, vel, acc, jerk, h_two)

    wait(recv_sem, part_two, 6, 9)
    total = part_two[0]
    for s in range(1, BLOCKS):
        total = total + part_two[s]
    total_two[slice_at] = total
    to_slices(lambda peer: total_two.at[slice_at], total_two, 6, 10)
    for sem, buffer, rows in (
        (0, got_pick, 6), (1, src_one, 8), (2, all_pick, 6), (3, got_base, 16), (4, all_base, 16), (5, src_two, 8),
        (6, part_one, 6), (7, updated, 8), (8, total_one, 6), (9, part_two, 6),
    ):
        wait(send_sem, buffer, rows, sem)
    wait(recv_sem, total_two, 6, 10)
    placed = put(jnp.concatenate([total_two[q] for q in range(SLICES)], axis=1), match_two[...])
    was_hit = hit_two > 0.5
    a_new, j_new = placed[0:3], placed[3:6]
    x_new, v_new = corrector_rest(x_base, v_base, a_new, j_new, h_two)
    out_pos[...] = jnp.where(was_hit, x_new, pos)
    out_vel[...] = jnp.where(was_hit, v_new, vel)
    out_acc[...] = jnp.where(was_hit, a_new, acc)
    out_jerk[...] = jnp.where(was_hit, j_new, jerk)
    wait(send_sem, total_two, 6, 10)


def write_out(pos, vel, acc, jerk, out_pos, out_vel, out_acc, out_jerk, sem):
    pairs = ((pos, out_pos), (vel, out_vel), (acc, out_acc), (jerk, out_jerk))
    copies = [pltpu.make_async_copy(a, b, sem.at[i]) for i, (a, b) in enumerate(pairs)]
    for copy in copies:
        copy.start()
    for copy in copies:
        copy.wait()


def body(position, velocity, acceleration, star_jerk, star_mass, time_last, first_active, second_active):
    vmem = pl.BlockSpec(memory_space=pltpu.VMEM)
    out = jax.ShapeDtypeStruct(position.shape, F32)
    held = pltpu.VMEM(position.shape, F32)
    slices = lambda rows, lanes=LANES: pltpu.VMEM((SLICES, rows, lanes), F32)
    blocks = lambda rows: pltpu.VMEM((BLOCKS, rows, LANES), F32)
    fields = pl.pallas_call(
        kernel,
        out_shape=(held,) * 4,
        in_specs=[pl.BlockSpec(memory_space=pltpu.HBM)] * 8,
        out_specs=(vmem,) * 4,
        scratch_shapes=[
            pltpu.VMEM((OWN, ACT), BF16),
            pltpu.VMEM((OWN, ACT), BF16),
            pltpu.VMEM((LANES, ACT), BF16),
            pltpu.VMEM((8, OWN), F32),
            pltpu.VMEM((6, LANES, LANES), F32),
            pltpu.VMEM((6, LANES, LANES), F32),
            slices(8),
            slices(16),
            pltpu.VMEM((16, LANES), F32),
            slices(8),
            slices(16),
            slices(8, OWN),
            slices(8, OWN),
            blocks(8),
            blocks(16),
            blocks(8),
            blocks(8),
            slices(8),
            slices(8),
            slices(8),
            *[pltpu.VMEM(position.shape, F32)] * 4,
            *[pltpu.VMEM((4, LANES), F32)] * 2,
            *[pltpu.VMEM((SLICES, LANES), jnp.int32)] * 2,
            pltpu.SemaphoreType.DMA((8,)),
            pltpu.SemaphoreType.DMA((11,)),
            pltpu.SemaphoreType.DMA((11,)),
        ],
        compiler_params=pltpu.CompilerParams(
            collective_id=0, has_side_effects=True, vmem_limit_bytes=63 * 1024 * 1024
        ),
    )(
        position,
        velocity,
        acceleration,
        star_jerk,
        star_mass.reshape(4, LANES),
        time_last.reshape(4, LANES),
        first_active.reshape(SLICES, LANES),
        second_active.reshape(SLICES, LANES),
    )
    return pl.pallas_call(
        write_out,
        out_shape=(out,) * 4,
        in_specs=[vmem] * 4,
        out_specs=(pl.BlockSpec(memory_space=pl.ANY),) * 4,
        scratch_shapes=[pltpu.SemaphoreType.DMA((4,))],
    )(*[pltpu.with_memory_space_constraint(f, pltpu.VMEM) for f in fields])


def solution(mesh):
    split = P(None, ("row", "rep"))
    flat = P(("row", "rep"))
    return jax.shard_map(
        body,
        mesh=mesh,
        in_specs=(split,) * 4 + (flat,) * 2 + (P(),) * 2,
        out_specs=(split,) * 4,
        check_vma=False,
    )
```

```python
import functools

import jax
import jax.numpy as jnp
from jax import lax
from jax.experimental import pallas as pl
from jax.experimental.pallas import tpu as pltpu
from jax.sharding import PartitionSpec as P

MESH = pl.DeviceIdType.MESH
F32 = jnp.float32
BF16 = jnp.bfloat16
EPS_SQ = 0.0004
T_ONE = 0.0
T_TWO = 0.03125
ACT = 2048
OWN = 512
LANES = 128
SLICES = 16
BLOCKS = 32


def place():
    row, rep = lax.axis_index("row"), lax.axis_index("rep")
    slice_at = (row // 8) * 2 + row % 2
    block_at = (rep // 2) * 8 + (rep % 2) * 4 + (row // 2) % 4
    return slice_at, block_at


def peers(slice_at, block_at):
    z, core = slice_at // 2, slice_at % 2
    x, y = block_at // 8, block_at % 8
    row = z * 8 + (y % 4) * 2 + core
    rep = x * 2 + y // 4
    near = (4, 3, 5, 2, 6, 1, 7, 0)
    zs = [(z + k) % 8 for k in near]
    ys = [(y + k) % 8 for k in near]
    xs = [(x + k) % 4 for k in (2, 1, 3, 0)]
    rows = [z * 8 + core + (k % 4) * 2 for k in ys]
    reps = [k // 4 for k in ys]
    others = [(k * 2 + side, (k * 8 + (y % 4) * 2 + side, rep)) for k in zs for side in (1 - core, core)]
    blocks = [(xs[i] * 8 + ys[j], (rows[j], xs[i] * 2 + reps[j])) for i in range(4) for j in range(8)]
    return others[:-1], blocks[:-1]


def split_rows(rows):
    high = rows.astype(BF16).astype(F32)
    rest = rows - high
    middle = rest.astype(BF16).astype(F32)
    low = rest - middle
    return jnp.concatenate([high, middle, low, jnp.zeros_like(rows)], axis=0).astype(BF16)


def join_rows(parts):
    return parts[0:8] + (parts[8:16] + parts[16:24])


def pick(rows, match):
    return join_rows(jnp.dot(split_rows(rows), match, preferred_element_type=F32))


def put(rows, match):
    dims = (((1,), (1,)), ((), ()))
    return join_rows(lax.dot_general(split_rows(rows), match, dims, preferred_element_type=F32))


def predict(x, v, a, j, h):
    return (x + h * (v + h * (0.5 * a + h * j / 6.0)), v + h * (a + h * 0.5 * j))


def corrector_base(x, v, a, j, h):
    v_base = v + 0.5 * h * a + h * h * j / 12.0
    x_base = x + 0.5 * h * (v + v_base) + h * h * a / 12.0
    return x_base, v_base


def corrector_rest(x_base, v_base, a_new, j_new, h):
    v_new = v_base + 0.5 * h * a_new - h * h * j_new / 12.0
    x_new = x_base + (h * h / 6.0) * a_new - (h * h * h / 24.0) * j_new
    return x_new, v_new


def forces(i_rows, source, extra, i_wide, sums):
    columns = jnp.transpose(i_rows)
    for c in range(6):
        i_wide[c] = jnp.broadcast_to(columns[:, c : c + 1], (LANES, LANES))
    groups = 4

    def add_pairs(star, total, src):
        dx, dy, dz = src[0] - star[0], src[1] - star[1], src[2] - star[2]
        ux, uy, uz = src[3] - star[3], src[4] - star[4], src[5] - star[5]
        inverse = lax.rsqrt(dx * dx + dy * dy + (dz * dz + EPS_SQ))
        inv_sq = inverse * inverse
        weight = (src[6] * inverse) * inv_sq
        radial = (dx * ux + dy * uy + dz * uz) * inv_sq
        turn = weight * (3.0 * radial)
        return (
            total[0] + weight * dx,
            total[1] + weight * dy,
            total[2] + weight * dz,
            total[3] + (weight * ux - turn * dx),
            total[4] + (weight * uy - turn * dy),
            total[5] + (weight * uz - turn * dz),
        )

    def some_stars(g, _):
        base = pl.multiple_of(g * (8 * groups), 8 * groups)
        stars = [[i_wide[c, pl.ds(base + 8 * k, 8), :] for c in range(6)] for k in range(groups)]

        def some_sources(t, totals):
            lane = pl.multiple_of((t % 4) * LANES, LANES)
            src = [
                jnp.broadcast_to(source[t // 4, c : c + 1, pl.ds(lane, LANES)], (8, LANES))
                for c in range(7)
            ]
            return tuple(add_pairs(stars[k], totals[k], src) for k in range(groups))

        zero = jnp.zeros((8, LANES), F32)
        totals = lax.fori_loop(0, 64, some_sources, ((zero,) * 6,) * groups, unroll=16)
        if extra is not None:
            src = [jnp.broadcast_to(extra[c : c + 1, :], (8, LANES)) for c in range(7)]
            totals = tuple(add_pairs(stars[k], totals[k], src) for k in range(groups))
        for k in range(groups):
            for c in range(6):
                sums[c, pl.ds(base + 8 * k, 8), :] = totals[k][c]
        return 0

    lax.fori_loop(0, LANES // (8 * groups), some_stars, 0)
    lane = lax.broadcasted_iota(jnp.int32, (LANES, LANES), 1)
    columns = jnp.zeros((LANES, LANES), F32)
    for c in range(6):
        columns = jnp.where(lane == c, jnp.sum(sums[c], axis=1, keepdims=True), columns)
    return jnp.transpose(columns)[0:8]


def kernel(
    pos_hbm, vel_hbm, acc_hbm, jerk_hbm, mass_hbm, time_hbm, first_hbm, second_hbm,
    out_pos, out_vel, out_acc, out_jerk,
    match_one, match_two, match_both, rows_scr, i_wide, sums,
    pick_one, pick_base, pick_two, base_mine,
    got_pick, got_base, got_two, src_one, src_two, all_pick, all_base, all_two,
    part_one, part_two, updated, total_one, total_two,
    pos_ref, vel_ref, acc_ref, jerk_ref, mass_ref, time_ref, first_ref, second_ref,
    load_sem, send_sem, recv_sem,
):
    slice_at, block_at = place()
    loads = [
        pltpu.make_async_copy(source, into, load_sem.at[i])
        for i, (source, into) in enumerate((
            (first_hbm, first_ref), (pos_hbm, pos_ref), (vel_hbm, vel_ref), (acc_hbm, acc_ref), (jerk_hbm, jerk_ref),
            (mass_hbm, mass_ref), (time_hbm, time_ref), (second_hbm, second_ref),
        ))
    ]
    for load in loads:
        load.start()

    barrier = pltpu.get_barrier_semaphore()

    other_slices, other_blocks = peers(slice_at, block_at)

    for _, to in other_blocks + other_slices:
        pl.semaphore_signal(barrier, inc=1, device_id=to, device_id_type=MESH)

    def to_slices(source_of, into, rows, sem):
        for peer, to in other_slices:
            pltpu.make_async_remote_copy(
                src_ref=source_of(peer).at[pl.ds(0, rows)],
                dst_ref=into.at[slice_at, pl.ds(0, rows)],
                send_sem=send_sem.at[sem],
                recv_sem=recv_sem.at[sem],
                device_id=to,
                device_id_type=MESH,
            ).start()

    def to_blocks(into, rows, sem):
        mine = into.at[block_at, pl.ds(0, rows)]
        for _, to in other_blocks:
            pltpu.make_async_remote_copy(
                src_ref=mine,
                dst_ref=mine,
                send_sem=send_sem.at[sem],
                recv_sem=recv_sem.at[sem],
                device_id=to,
                device_id_type=MESH,
            ).start()

    def wait(sems, buffer, rows, sem):
        whole = buffer.at[pl.ds(0, buffer.shape[0] - 1), pl.ds(0, rows)]
        pltpu.make_async_copy(whole, whole, sems.at[sem]).wait()

    for load in loads:
        load.wait()
    pos, vel, acc, jerk = pos_ref[...], vel_ref[...], acc_ref[...], jerk_ref[...]
    time = jnp.concatenate([time_ref[k : k + 1, :] for k in range(4)], axis=1)
    mass = jnp.concatenate([mass_ref[k : k + 1, :] for k in range(4)], axis=1)
    base_id = (lax.axis_index("row") * 8 + lax.axis_index("rep")) * OWN
    owned = lax.broadcasted_iota(jnp.int32, (OWN, LANES), 0) + base_id

    def fill_match(match, ids):
        for q in range(SLICES):
            hit = jnp.broadcast_to(ids[q : q + 1, :], (OWN, LANES)) == owned
            match[:, q * LANES : (q + 1) * LANES] = jnp.where(hit, 1.0, 0.0).astype(BF16)

    fill_match(match_one, first_ref)
    h_one = T_ONE - time
    pred_pos, pred_vel = predict(pos, vel, acc, jerk, h_one)
    rows_scr[0:3, :] = pred_pos
    rows_scr[3:6, :] = pred_vel
    rows_scr[6:7, :] = mass
    rows_scr[7:8, :] = jnp.zeros_like(mass)
    rows = rows_scr[...]
    src_one[slice_at] = rows
    picked = pick(rows, match_one[...])
    for q in range(SLICES):
        pick_one[q] = picked[:, q * LANES : (q + 1) * LANES]
    got_pick[slice_at] = pick_one[slice_at]

    x_base, v_base = corrector_base(pos, vel, acc, jerk, h_one)
    rows_scr[0:3, :] = x_base
    rows_scr[3:6, :] = v_base
    rows_scr[6:7, :] = h_one
    rows_scr[7:8, :] = mass
    picked = pick(rows_scr[...], match_one[...])
    for q in range(SLICES):
        pick_base[q] = picked[:, q * LANES : (q + 1) * LANES]
    got_base[slice_at] = pick_base[slice_at]

    pl.semaphore_wait(barrier, SLICES + BLOCKS - 2)
    to_slices(lambda peer: pick_one.at[peer], got_pick, 6, 0)
    to_slices(lambda peer: pick_base.at[peer], got_base, 8, 3)
    to_slices(lambda peer: src_one.at[slice_at], src_one, 8, 1)

    fill_match(match_two, second_ref)
    pred_pos, pred_vel = predict(pos, vel, acc, jerk, T_TWO - time)
    rows_scr[0:3, :] = pred_pos
    rows_scr[3:6, :] = pred_vel
    rows_scr[6:7, :] = mass
    rows_scr[7:8, :] = jnp.zeros_like(mass)
    picked = pick(rows_scr[...], match_two[...])
    for q in range(SLICES):
        pick_two[q] = picked[:, q * LANES : (q + 1) * LANES]
    got_two[slice_at] = pick_two[slice_at]
    to_slices(lambda peer: pick_two.at[peer], got_two, 6, 11)
    ones = jnp.ones((16, ACT), BF16)
    dims = (((1,), (1,)), ((), ()))
    hit_one = lax.dot_general(ones, match_one[...], dims, preferred_element_type=F32)[0:1]
    hit_two = lax.dot_general(ones, match_two[...], dims, preferred_element_type=F32)[0:1]
    rows_scr[6:7, :] = jnp.where(hit_one > 0.5, 0.0, mass)
    src_two[slice_at] = rows_scr[...]

    wait(recv_sem, got_pick, 6, 0)
    total = got_pick[0]
    for q in range(1, SLICES):
        total = total + got_pick[q]
    all_pick[block_at] = total
    to_blocks(all_pick, 6, 2)

    mine = jnp.broadcast_to(second_ref[pl.ds(slice_at, 1), :].astype(F32), (LANES, LANES))
    mine = jnp.transpose(mine)
    for q in range(SLICES):
        theirs = jnp.broadcast_to(first_ref[q : q + 1, :].astype(F32), (LANES, LANES))
        hit = jnp.where(mine == theirs, 1.0, 0.0).astype(BF16)
        match_both[:, q * LANES : (q + 1) * LANES] = hit

    wait(recv_sem, got_base, 8, 3)
    total = got_base[0]
    for q in range(1, SLICES):
        total = total + got_base[q]
    all_base[block_at] = total
    to_blocks(all_base, 8, 4)

    wait(recv_sem, src_one, 8, 1)
    wait(recv_sem, all_pick, 6, 2)
    stars_one = all_pick[0]
    for s in range(1, BLOCKS):
        stars_one = stars_one + all_pick[s]
    part_one[block_at] = forces(stars_one, src_one, None, i_wide, sums)
    to_blocks(part_one, 6, 6)
    wait(recv_sem, got_two, 6, 11)
    total = got_two[0]
    for q in range(1, SLICES):
        total = total + got_two[q]
    all_two[block_at] = total
    to_blocks(all_two, 6, 12)
    to_slices(lambda peer: src_two.at[slice_at], src_two, 8, 5)

    wait(recv_sem, all_base, 8, 4)
    base = all_base[0]
    for s in range(1, BLOCKS):
        base = base + all_base[s]
    base_mine[...] = base
    wait(recv_sem, part_one, 6, 6)
    total = part_one[0]
    for s in range(1, BLOCKS):
        total = total + part_one[s]
    h = base_mine[6:7, :]
    a_new, j_new = total[0:3], total[3:6]
    x_new, v_new = corrector_rest(base_mine[0:3, :], base_mine[3:6, :], a_new, j_new, h)
    pred_pos, pred_vel = predict(x_new, v_new, a_new, j_new, T_TWO - T_ONE)
    updated[slice_at, 0:3, :] = pred_pos
    updated[slice_at, 3:6, :] = pred_vel
    updated[slice_at, 6:7, :] = base_mine[7:8, :]
    updated[slice_at, 7:8, :] = jnp.ones_like(h)
    to_slices(lambda peer: updated.at[slice_at], updated, 8, 7)
    total_one[slice_at] = total
    to_slices(lambda peer: total_one.at[slice_at], total_one, 6, 8)

    wait(recv_sem, all_two, 6, 12)
    stars_two = all_two[0]
    for s in range(1, BLOCKS):
        stars_two = stars_two + all_two[s]
    wait(recv_sem, src_two, 8, 5)
    wait(recv_sem, updated, 8, 7)
    moved = jnp.concatenate([updated[q] for q in range(SLICES)], axis=1)
    moved = put(moved, match_both[...])
    stars_two = jnp.where(moved[7:8] > 0.5, moved, stars_two)
    extra = updated[block_at // 2]
    lane = lax.broadcasted_iota(jnp.int32, (8, LANES), 1)
    row = lax.broadcasted_iota(jnp.int32, (8, LANES), 0)
    extra = jnp.where((row == 6) & (lane // 64 != block_at % 2), 0.0, extra)
    part_two[block_at] = forces(stars_two, src_two, extra, i_wide, sums)
    to_blocks(part_two, 6, 9)

    wait(recv_sem, total_one, 6, 8)
    placed = put(jnp.concatenate([total_one[q] for q in range(SLICES)], axis=1), match_one[...])
    was_hit = hit_one > 0.5
    a_new, j_new = placed[0:3], placed[3:6]
    x_new, v_new = corrector_rest(x_base, v_base, a_new, j_new, h_one)
    pos = jnp.where(was_hit, x_new, pos)
    vel = jnp.where(was_hit, v_new, vel)
    acc = jnp.where(was_hit, a_new, acc)
    jerk = jnp.where(was_hit, j_new, jerk)
    h_two = T_TWO - jnp.where(was_hit, T_ONE, time)
    x_base, v_base = corrector_base(pos, vel, acc, jerk, h_two)

    wait(recv_sem, part_two, 6, 9)
    total = part_two[0]
    for s in range(1, BLOCKS):
        total = total + part_two[s]
    total_two[slice_at] = total
    to_slices(lambda peer: total_two.at[slice_at], total_two, 6, 10)
    for sem, buffer, rows in (
        (0, got_pick, 6), (1, src_one, 8), (2, all_pick, 6), (3, got_base, 8), (4, all_base, 8), (5, src_two, 8),
        (6, part_one, 6), (7, updated, 8), (8, total_one, 6), (9, part_two, 6),
        (11, got_two, 6), (12, all_two, 6),
    ):
        wait(send_sem, buffer, rows, sem)
    wait(recv_sem, total_two, 6, 10)
    placed = put(jnp.concatenate([total_two[q] for q in range(SLICES)], axis=1), match_two[...])
    was_hit = hit_two > 0.5
    a_new, j_new = placed[0:3], placed[3:6]
    x_new, v_new = corrector_rest(x_base, v_base, a_new, j_new, h_two)
    out_pos[...] = jnp.where(was_hit, x_new, pos)
    out_vel[...] = jnp.where(was_hit, v_new, vel)
    out_acc[...] = jnp.where(was_hit, a_new, acc)
    out_jerk[...] = jnp.where(was_hit, j_new, jerk)
    wait(send_sem, total_two, 6, 10)


def write_out(pos, vel, acc, jerk, out_pos, out_vel, out_acc, out_jerk, sem):
    pairs = ((pos, out_pos), (vel, out_vel), (acc, out_acc), (jerk, out_jerk))
    copies = [pltpu.make_async_copy(a, b, sem.at[i]) for i, (a, b) in enumerate(pairs)]
    for copy in copies:
        copy.start()
    for copy in copies:
        copy.wait()


def body(position, velocity, acceleration, star_jerk, star_mass, time_last, first_active, second_active):
    vmem = pl.BlockSpec(memory_space=pltpu.VMEM)
    out = jax.ShapeDtypeStruct(position.shape, F32)
    held = pltpu.VMEM(position.shape, F32)
    slices = lambda rows, lanes=LANES: pltpu.VMEM((SLICES, rows, lanes), F32)
    blocks = lambda rows: pltpu.VMEM((BLOCKS, rows, LANES), F32)
    fields = pl.pallas_call(
        kernel,
        out_shape=(held,) * 4,
        in_specs=[pl.BlockSpec(memory_space=pltpu.HBM)] * 8,
        out_specs=(vmem,) * 4,
        scratch_shapes=[
            pltpu.VMEM((OWN, ACT), BF16),
            pltpu.VMEM((OWN, ACT), BF16),
            pltpu.VMEM((LANES, ACT), BF16),
            pltpu.VMEM((8, OWN), F32),
            pltpu.VMEM((6, LANES, LANES), F32),
            pltpu.VMEM((6, LANES, LANES), F32),
            slices(8),
            slices(8),
            slices(8),
            pltpu.VMEM((8, LANES), F32),
            slices(8),
            slices(8),
            slices(8),
            slices(8, OWN),
            slices(8, OWN),
            blocks(8),
            blocks(8),
            blocks(8),
            blocks(8),
            blocks(8),
            slices(8),
            slices(8),
            slices(8),
            *[pltpu.VMEM(position.shape, F32)] * 4,
            *[pltpu.VMEM((4, LANES), F32)] * 2,
            *[pltpu.VMEM((SLICES, LANES), jnp.int32)] * 2,
            pltpu.SemaphoreType.DMA((8,)),
            pltpu.SemaphoreType.DMA((13,)),
            pltpu.SemaphoreType.DMA((13,)),
        ],
        compiler_params=pltpu.CompilerParams(
            collective_id=0, has_side_effects=True, vmem_limit_bytes=63 * 1024 * 1024
        ),
    )(
        position,
        velocity,
        acceleration,
        star_jerk,
        star_mass.reshape(4, LANES),
        time_last.reshape(4, LANES),
        first_active.reshape(SLICES, LANES),
        second_active.reshape(SLICES, LANES),
    )
    return pl.pallas_call(
        write_out,
        out_shape=(out,) * 4,
        in_specs=[vmem] * 4,
        out_specs=(pl.BlockSpec(memory_space=pl.ANY),) * 4,
        scratch_shapes=[pltpu.SemaphoreType.DMA((4,))],
    )(*[pltpu.with_memory_space_constraint(f, pltpu.VMEM) for f in fields])


def solution(mesh):
    split = P(None, ("row", "rep"))
    flat = P(("row", "rep"))
    return jax.shard_map(
        body,
        mesh=mesh,
        in_specs=(split,) * 4 + (flat,) * 2 + (P(),) * 2,
        out_specs=(split,) * 4,
        check_vma=False,
    )
```

```python
import functools

import jax
import jax.numpy as jnp
from jax import lax
from jax.experimental import pallas as pl
from jax.experimental.pallas import tpu as pltpu
from jax.sharding import PartitionSpec as P

MESH = pl.DeviceIdType.MESH
F32 = jnp.float32
BF16 = jnp.bfloat16
EPS_SQ = 0.0004
T_ONE = 0.0
T_TWO = 0.03125
ACT = 2048
OWN = 512
LANES = 128
SLICES = 16
BLOCKS = 32


def place():
    row, rep = lax.axis_index("row"), lax.axis_index("rep")
    slice_at = (row // 8) * 2 + row % 2
    block_at = (rep // 2) * 8 + (rep % 2) * 4 + (row // 2) % 4
    return slice_at, block_at


def peers(slice_at, block_at):
    z, core = slice_at // 2, slice_at % 2
    x, y = block_at // 8, block_at % 8
    row = z * 8 + (y % 4) * 2 + core
    rep = x * 2 + y // 4
    near = (4, 3, 5, 2, 6, 1, 7, 0)
    zs = [(z + k) % 8 for k in near]
    ys = [(y + k) % 8 for k in near]
    xs = [(x + k) % 4 for k in (2, 1, 3, 0)]
    rows = [z * 8 + core + (k % 4) * 2 for k in ys]
    reps = [k // 4 for k in ys]
    others = [(k * 2 + side, (k * 8 + (y % 4) * 2 + side, rep)) for k in zs for side in (1 - core, core)]
    blocks = [(xs[i] * 8 + ys[j], (rows[j], xs[i] * 2 + reps[j])) for j in range(8) for i in range(4)]
    return others[:-1], blocks[:-1]


def split_rows(rows):
    high = rows.astype(BF16).astype(F32)
    rest = rows - high
    middle = rest.astype(BF16).astype(F32)
    low = rest - middle
    return jnp.concatenate([high, middle, low, jnp.zeros_like(rows)], axis=0).astype(BF16)


def join_rows(parts):
    return parts[0:8] + (parts[8:16] + parts[16:24])


def pick(rows, match):
    return join_rows(jnp.dot(split_rows(rows), match, preferred_element_type=F32))


def put(rows, match):
    dims = (((1,), (1,)), ((), ()))
    return join_rows(lax.dot_general(split_rows(rows), match, dims, preferred_element_type=F32))


def predict(x, v, a, j, h):
    return (x + h * (v + h * (0.5 * a + h * j / 6.0)), v + h * (a + h * 0.5 * j))


def corrector_base(x, v, a, j, h):
    v_base = v + 0.5 * h * a + h * h * j / 12.0
    x_base = x + 0.5 * h * (v + v_base) + h * h * a / 12.0
    return x_base, v_base


def corrector_rest(x_base, v_base, a_new, j_new, h):
    v_new = v_base + 0.5 * h * a_new - h * h * j_new / 12.0
    x_new = x_base + (h * h / 6.0) * a_new - (h * h * h / 24.0) * j_new
    return x_new, v_new


def forces(i_rows, source, extra, i_wide, sums):
    columns = jnp.transpose(i_rows)
    for c in range(6):
        i_wide[c] = jnp.broadcast_to(columns[:, c : c + 1], (LANES, LANES))
    groups = 4

    def add_pairs(star, total, src):
        dx, dy, dz = src[0] - star[0], src[1] - star[1], src[2] - star[2]
        ux, uy, uz = src[3] - star[3], src[4] - star[4], src[5] - star[5]
        inverse = lax.rsqrt(dx * dx + dy * dy + (dz * dz + EPS_SQ))
        inv_sq = inverse * inverse
        weight = (src[6] * inverse) * inv_sq
        radial = (dx * ux + dy * uy + dz * uz) * (3.0 * inv_sq)
        return (
            total[0] + weight * dx,
            total[1] + weight * dy,
            total[2] + weight * dz,
            total[3] + weight * (ux - radial * dx),
            total[4] + weight * (uy - radial * dy),
            total[5] + weight * (uz - radial * dz),
        )

    def some_stars(g, _):
        base = pl.multiple_of(g * (8 * groups), 8 * groups)
        stars = [[i_wide[c, pl.ds(base + 8 * k, 8), :] for c in range(6)] for k in range(groups)]

        def some_sources(t, totals):
            lane = pl.multiple_of((t % 4) * LANES, LANES)
            src = [
                jnp.broadcast_to(source[t // 4, c : c + 1, pl.ds(lane, LANES)], (8, LANES))
                for c in range(7)
            ]
            return tuple(add_pairs(stars[k], totals[k], src) for k in range(groups))

        zero = jnp.zeros((8, LANES), F32)
        totals = lax.fori_loop(0, 64, some_sources, ((zero,) * 6,) * groups, unroll=16)
        if extra is not None:
            src = [jnp.broadcast_to(extra[c : c + 1, :], (8, LANES)) for c in range(7)]
            totals = tuple(add_pairs(stars[k], totals[k], src) for k in range(groups))
        for k in range(groups):
            for c in range(6):
                sums[c, pl.ds(base + 8 * k, 8), :] = totals[k][c]
        return 0

    lax.fori_loop(0, LANES // (8 * groups), some_stars, 0)
    lane = lax.broadcasted_iota(jnp.int32, (LANES, LANES), 1)
    columns = jnp.zeros((LANES, LANES), F32)
    for c in range(6):
        columns = jnp.where(lane == c, jnp.sum(sums[c], axis=1, keepdims=True), columns)
    return jnp.transpose(columns)[0:8]


def kernel(
    pos_hbm, vel_hbm, acc_hbm, jerk_hbm, mass_hbm, time_hbm, first_hbm, second_hbm,
    out_pos, out_vel, out_acc, out_jerk,
    match_one, match_two, match_both, rows_scr, i_wide, sums,
    pick_one, pick_base, pick_two, base_mine,
    got_pick, got_base, got_two, src_one, src_two, all_pick, all_base, all_two,
    part_one, part_two, updated, total_one, total_two,
    pos_ref, vel_ref, acc_ref, jerk_ref, mass_ref, time_ref, first_ref, second_ref,
    load_sem, send_sem, recv_sem,
):
    slice_at, block_at = place()
    loads = [
        pltpu.make_async_copy(source, into, load_sem.at[i])
        for i, (source, into) in enumerate((
            (first_hbm, first_ref), (pos_hbm, pos_ref), (vel_hbm, vel_ref), (acc_hbm, acc_ref), (jerk_hbm, jerk_ref),
            (mass_hbm, mass_ref), (time_hbm, time_ref), (second_hbm, second_ref),
        ))
    ]
    barrier = pltpu.get_barrier_semaphore()

    other_slices, other_blocks = peers(slice_at, block_at)

    for _, to in other_blocks:
        pl.semaphore_signal(barrier, inc=1, device_id=to, device_id_type=MESH)
    for load in loads:
        load.start()
    for _, to in other_slices:
        pl.semaphore_signal(barrier, inc=1, device_id=to, device_id_type=MESH)

    def to_slices(source_of, into, rows, sem):
        for peer, to in other_slices:
            pltpu.make_async_remote_copy(
                src_ref=source_of(peer).at[pl.ds(0, rows)],
                dst_ref=into.at[slice_at, pl.ds(0, rows)],
                send_sem=send_sem.at[sem],
                recv_sem=recv_sem.at[sem],
                device_id=to,
                device_id_type=MESH,
            ).start()

    def to_blocks(into, rows, sem):
        mine = into.at[block_at, pl.ds(0, rows)]
        for _, to in other_blocks:
            pltpu.make_async_remote_copy(
                src_ref=mine,
                dst_ref=mine,
                send_sem=send_sem.at[sem],
                recv_sem=recv_sem.at[sem],
                device_id=to,
                device_id_type=MESH,
            ).start()

    def wait(sems, buffer, rows, sem):
        whole = buffer.at[pl.ds(0, buffer.shape[0] - 1), pl.ds(0, rows)]
        pltpu.make_async_copy(whole, whole, sems.at[sem]).wait()

    for load in loads:
        load.wait()
    pos, vel, acc, jerk = pos_ref[...], vel_ref[...], acc_ref[...], jerk_ref[...]
    time = jnp.concatenate([time_ref[k : k + 1, :] for k in range(4)], axis=1)
    mass = jnp.concatenate([mass_ref[k : k + 1, :] for k in range(4)], axis=1)
    base_id = (lax.axis_index("row") * 8 + lax.axis_index("rep")) * OWN
    owned = lax.broadcasted_iota(jnp.int32, (OWN, LANES), 0) + base_id

    def fill_match(match, ids):
        for q in range(SLICES):
            hit = jnp.broadcast_to(ids[q : q + 1, :], (OWN, LANES)) == owned
            match[:, q * LANES : (q + 1) * LANES] = jnp.where(hit, 1.0, 0.0).astype(BF16)

    fill_match(match_one, first_ref)
    h_one = T_ONE - time
    pred_pos, pred_vel = predict(pos, vel, acc, jerk, h_one)
    rows_scr[0:3, :] = pred_pos
    rows_scr[3:6, :] = pred_vel
    rows_scr[6:7, :] = mass
    rows_scr[7:8, :] = jnp.zeros_like(mass)
    rows = rows_scr[...]
    src_one[slice_at] = rows
    picked = pick(rows, match_one[...])
    for q in range(SLICES):
        pick_one[q] = picked[:, q * LANES : (q + 1) * LANES]
    got_pick[slice_at] = pick_one[slice_at]

    x_base, v_base = corrector_base(pos, vel, acc, jerk, h_one)
    rows_scr[0:3, :] = x_base
    rows_scr[3:6, :] = v_base
    rows_scr[6:7, :] = h_one
    rows_scr[7:8, :] = mass
    picked = pick(rows_scr[...], match_one[...])
    for q in range(SLICES):
        pick_base[q] = picked[:, q * LANES : (q + 1) * LANES]
    got_base[slice_at] = pick_base[slice_at]

    pl.semaphore_wait(barrier, SLICES + BLOCKS - 2)
    to_slices(lambda peer: pick_one.at[peer], got_pick, 6, 0)
    to_slices(lambda peer: pick_base.at[peer], got_base, 8, 3)
    to_slices(lambda peer: src_one.at[slice_at], src_one, 8, 1)

    fill_match(match_two, second_ref)
    pred_pos, pred_vel = predict(pos, vel, acc, jerk, T_TWO - time)
    rows_scr[0:3, :] = pred_pos
    rows_scr[3:6, :] = pred_vel
    rows_scr[6:7, :] = mass
    rows_scr[7:8, :] = jnp.zeros_like(mass)
    picked = pick(rows_scr[...], match_two[...])
    for q in range(SLICES):
        pick_two[q] = picked[:, q * LANES : (q + 1) * LANES]
    got_two[slice_at] = pick_two[slice_at]
    to_slices(lambda peer: pick_two.at[peer], got_two, 6, 11)
    ones = jnp.ones((16, ACT), BF16)
    dims = (((1,), (1,)), ((), ()))
    hit_one = lax.dot_general(ones, match_one[...], dims, preferred_element_type=F32)[0:1]
    hit_two = lax.dot_general(ones, match_two[...], dims, preferred_element_type=F32)[0:1]
    rows_scr[6:7, :] = jnp.where(hit_one > 0.5, 0.0, mass)
    src_two[slice_at] = rows_scr[...]

    wait(recv_sem, got_pick, 6, 0)
    total = got_pick[0]
    for q in range(1, SLICES):
        total = total + got_pick[q]
    all_pick[block_at] = total
    to_blocks(all_pick, 6, 2)

    mine = jnp.broadcast_to(second_ref[pl.ds(slice_at, 1), :].astype(F32), (LANES, LANES))
    mine = jnp.transpose(mine)
    for q in range(SLICES):
        theirs = jnp.broadcast_to(first_ref[q : q + 1, :].astype(F32), (LANES, LANES))
        hit = jnp.where(mine == theirs, 1.0, 0.0).astype(BF16)
        match_both[:, q * LANES : (q + 1) * LANES] = hit

    wait(recv_sem, got_base, 8, 3)
    total = got_base[0]
    for q in range(1, SLICES):
        total = total + got_base[q]
    all_base[block_at] = total
    to_blocks(all_base, 8, 4)

    wait(recv_sem, src_one, 8, 1)
    wait(recv_sem, all_pick, 6, 2)
    stars_one = all_pick[0]
    for s in range(1, BLOCKS):
        stars_one = stars_one + all_pick[s]
    part_one[block_at] = forces(stars_one, src_one, None, i_wide, sums)
    to_blocks(part_one, 6, 6)
    wait(recv_sem, got_two, 6, 11)
    total = got_two[0]
    for q in range(1, SLICES):
        total = total + got_two[q]
    all_two[block_at] = total
    to_blocks(all_two, 6, 12)
    to_slices(lambda peer: src_two.at[slice_at], src_two, 8, 5)

    wait(recv_sem, all_base, 8, 4)
    base = all_base[0]
    for s in range(1, BLOCKS):
        base = base + all_base[s]
    base_mine[...] = base
    wait(recv_sem, part_one, 6, 6)
    total = part_one[0]
    for s in range(1, BLOCKS):
        total = total + part_one[s]
    h = base_mine[6:7, :]
    a_new, j_new = total[0:3], total[3:6]
    x_new, v_new = corrector_rest(base_mine[0:3, :], base_mine[3:6, :], a_new, j_new, h)
    pred_pos, pred_vel = predict(x_new, v_new, a_new, j_new, T_TWO - T_ONE)
    updated[slice_at, 0:3, :] = pred_pos
    updated[slice_at, 3:6, :] = pred_vel
    updated[slice_at, 6:7, :] = base_mine[7:8, :]
    updated[slice_at, 7:8, :] = jnp.ones_like(h)
    to_slices(lambda peer: updated.at[slice_at], updated, 8, 7)
    total_one[slice_at] = total

    wait(recv_sem, all_two, 6, 12)
    stars_two = all_two[0]
    for s in range(1, BLOCKS):
        stars_two = stars_two + all_two[s]
    wait(recv_sem, src_two, 8, 5)
    wait(recv_sem, updated, 8, 7)
    moved = jnp.concatenate([updated[q] for q in range(SLICES)], axis=1)
    moved = put(moved, match_both[...])
    stars_two = jnp.where(moved[7:8] > 0.5, moved, stars_two)
    extra = updated[block_at // 2]
    lane = lax.broadcasted_iota(jnp.int32, (8, LANES), 1)
    row = lax.broadcasted_iota(jnp.int32, (8, LANES), 0)
    extra = jnp.where((row == 6) & (lane // 64 != block_at % 2), 0.0, extra)
    part_two[block_at] = forces(stars_two, src_two, extra, i_wide, sums)
    to_blocks(part_two, 6, 9)
    to_slices(lambda peer: total_one.at[slice_at], total_one, 6, 8)

    wait(recv_sem, total_one, 6, 8)
    placed = put(jnp.concatenate([total_one[q] for q in range(SLICES)], axis=1), match_one[...])
    was_hit = hit_one > 0.5
    a_new, j_new = placed[0:3], placed[3:6]
    x_new, v_new = corrector_rest(x_base, v_base, a_new, j_new, h_one)
    pos = jnp.where(was_hit, x_new, pos)
    vel = jnp.where(was_hit, v_new, vel)
    acc = jnp.where(was_hit, a_new, acc)
    jerk = jnp.where(was_hit, j_new, jerk)
    h_two = T_TWO - jnp.where(was_hit, T_ONE, time)
    x_base, v_base = corrector_base(pos, vel, acc, jerk, h_two)

    wait(recv_sem, part_two, 6, 9)
    total = part_two[0]
    for s in range(1, BLOCKS):
        total = total + part_two[s]
    total_two[slice_at] = total
    to_slices(lambda peer: total_two.at[slice_at], total_two, 6, 10)
    for sem, buffer, rows in (
        (0, got_pick, 6), (1, src_one, 8), (2, all_pick, 6), (3, got_base, 8), (4, all_base, 8), (5, src_two, 8),
        (6, part_one, 6), (7, updated, 8), (8, total_one, 6), (9, part_two, 6),
        (11, got_two, 6), (12, all_two, 6),
    ):
        wait(send_sem, buffer, rows, sem)
    wait(recv_sem, total_two, 6, 10)
    placed = put(jnp.concatenate([total_two[q] for q in range(SLICES)], axis=1), match_two[...])
    was_hit = hit_two > 0.5
    a_new, j_new = placed[0:3], placed[3:6]
    x_new, v_new = corrector_rest(x_base, v_base, a_new, j_new, h_two)
    out_pos[...] = jnp.where(was_hit, x_new, pos)
    out_vel[...] = jnp.where(was_hit, v_new, vel)
    out_acc[...] = jnp.where(was_hit, a_new, acc)
    out_jerk[...] = jnp.where(was_hit, j_new, jerk)
    wait(send_sem, total_two, 6, 10)


def write_out(pos, vel, acc, jerk, out_pos, out_vel, out_acc, out_jerk, sem):
    pairs = ((pos, out_pos), (vel, out_vel), (acc, out_acc), (jerk, out_jerk))
    copies = [pltpu.make_async_copy(a, b, sem.at[i]) for i, (a, b) in enumerate(pairs)]
    for copy in copies:
        copy.start()
    for copy in copies:
        copy.wait()


def body(position, velocity, acceleration, star_jerk, star_mass, time_last, first_active, second_active):
    vmem = pl.BlockSpec(memory_space=pltpu.VMEM)
    out = jax.ShapeDtypeStruct(position.shape, F32)
    held = pltpu.VMEM(position.shape, F32)
    slices = lambda rows, lanes=LANES: pltpu.VMEM((SLICES, rows, lanes), F32)
    blocks = lambda rows: pltpu.VMEM((BLOCKS, rows, LANES), F32)
    fields = pl.pallas_call(
        kernel,
        out_shape=(held,) * 4,
        in_specs=[pl.BlockSpec(memory_space=pltpu.HBM)] * 8,
        out_specs=(vmem,) * 4,
        scratch_shapes=[
            pltpu.VMEM((OWN, ACT), BF16),
            pltpu.VMEM((OWN, ACT), BF16),
            pltpu.VMEM((LANES, ACT), BF16),
            pltpu.VMEM((8, OWN), F32),
            pltpu.VMEM((6, LANES, LANES), F32),
            pltpu.VMEM((6, LANES, LANES), F32),
            slices(8),
            slices(8),
            slices(8),
            pltpu.VMEM((8, LANES), F32),
            slices(8),
            slices(8),
            slices(8),
            slices(8, OWN),
            slices(8, OWN),
            blocks(8),
            blocks(8),
            blocks(8),
            blocks(8),
            blocks(8),
            slices(8),
            slices(8),
            slices(8),
            *[pltpu.VMEM(position.shape, F32)] * 4,
            *[pltpu.VMEM((4, LANES), F32)] * 2,
            *[pltpu.VMEM((SLICES, LANES), jnp.int32)] * 2,
            pltpu.SemaphoreType.DMA((8,)),
            pltpu.SemaphoreType.DMA((13,)),
            pltpu.SemaphoreType.DMA((13,)),
        ],
        compiler_params=pltpu.CompilerParams(
            collective_id=0, has_side_effects=True, vmem_limit_bytes=63 * 1024 * 1024
        ),
    )(
        position,
        velocity,
        acceleration,
        star_jerk,
        star_mass.reshape(4, LANES),
        time_last.reshape(4, LANES),
        first_active.reshape(SLICES, LANES),
        second_active.reshape(SLICES, LANES),
    )
    return pl.pallas_call(
        write_out,
        out_shape=(out,) * 4,
        in_specs=[vmem] * 4,
        out_specs=(pl.BlockSpec(memory_space=pl.ANY),) * 4,
        scratch_shapes=[pltpu.SemaphoreType.DMA((4,))],
    )(*[pltpu.with_memory_space_constraint(f, pltpu.VMEM) for f in fields])


def solution(mesh):
    split = P(None, ("row", "rep"))
    flat = P(("row", "rep"))
    return jax.shard_map(
        body,
        mesh=mesh,
        in_specs=(split,) * 4 + (flat,) * 2 + (P(),) * 2,
        out_specs=(split,) * 4,
        check_vma=False,
    )
```
